32 devices in a mesh: groups: 2 (over y), batch: 4 (over z), block: 2 (over x), rep: 2 (over core).
Axes of the slice: x: 2, y: 2, z: 4, core: 2. Of those that a mesh axis runs over, the one named last changes fastest.
Arguments:
- colloc: bfloat16 [128, 512, 384], P(('groups', 'batch', 'block', 'rep')), parts along dimension 0, may hold values from -6 to 6
- blocks: int32 [128, 3], P(('groups', 'batch', 'block', 'rep')), parts along dimension 0, may hold values from 0 to 31, as said below
- points: float32 [128, 3, 512], P(('groups', 'batch', 'block', 'rep')), parts along dimension 0, may hold values from -3 to 3
- centers: float32 [3, 8192], P(None, 'groups'), parts along dimension 1, may hold values from -3 to 3
- exponents: float32 [8192], P('groups'), parts along dimension 0, may hold values from 0.1 to 1
- density: bfloat16 [64, 7, 128, 128], P(('groups', 'batch', 'block')), parts along dimension 0, may hold values from -0.3046875 to 0.3046875
Outputs:
- exchange_band: bfloat16 [64, 7, 128, 128], P(('groups', 'batch', 'block', 'rep')), parts along dimension 0
The draws below stay inside these ranges and needn't reach their ends.
There are 2 independent parts, one for each index of `groups`. The reference program is written for one: setup_inputs(seed, part) draws one part's arguments, and reference() takes and returns one part's arrays. A program takes and returns all parts, laid end to end along the dimension named above; each array names one. Nothing has to cross between parts.
Inputs may be any that keep to these rules, and one draw needn't show every extreme that they name: Each batch lists 3 increasing row blocks that lie within 4 consecutive blocks; the batches of one device (t from d * 4 to d * 4 + 3) list distinct blocks. Among the blocks listed by the batches of one device, the largest number that share one value mod 8 is exactly 2.
All inputs are finite; a program needn't handle non-finite values.
Results may differ from the reference program's by a relative error of at most 0.012.
Values may be sent and summed in bfloat16 or wider, within the bound.
A program may use at most 64 MiB of HBM per device.

```python
import math
import jax
import jax.numpy as jnp
from jax import lax

BLK = 128
PTS = 512
L = 3
BATCH_DEV = 4
BLK_DEV = 4
SPAN = 4
BAND = 7
NBLK = 32
NBF = 4096
BATCHES = 64
N_BATCH = 4
N_BLOCK = 2
N_REP = 2


def draw_blocks(key, part):
    key = jax.random.fold_in(key, 11)
    devices = BATCHES // BATCH_DEV
    region = BATCH_DEV * SPAN
    first = jax.random.randint(jax.random.fold_in(key, 1), (devices,), 0, NBLK - region + 1)
    skipped = jax.random.randint(jax.random.fold_in(key, 2), (devices,), 0, SPAN)
    within = jnp.arange(L, dtype=jnp.int32)
    offsets = within[None, :] + (within[None, :] >= skipped[:, None]).astype(jnp.int32)
    order = jnp.arange(BATCH_DEV, dtype=jnp.int32) * SPAN
    listed = first[:, None, None] + order[None, :, None] + offsets[:, None, :]
    return listed.reshape(BATCHES, L).astype(jnp.int32)


def levels(key, extent, cuts, least, largest):
    gain, own = 1.0, jax.random.fold_in(key, 6)
    for position, blocks in cuts:
        draws = jnp.exp(jax.random.uniform(jax.random.fold_in(own, position), (blocks,), jnp.float32, least / len(cuts), largest / len(cuts)))
        gain = gain * jnp.repeat(draws, extent[position] // blocks).reshape([-1 if axis == position else 1 for axis in range(len(extent))])
    return gain


def normal_values(key, shape, spread, reach, shards=(), kind=jnp.bfloat16):
    array = spread * jax.random.normal(key, shape, jnp.float32)
    if shards:
        array = array * levels(key, shape, shards, -0.22, 0.18)
    return jnp.clip(array, -reach, reach).astype(kind)


def setup_inputs(seed: int = 0, part: int = 0) -> dict:
    keys = jax.random.split(jax.random.key(seed), 7)
    part_splits = jax.random.split(jax.random.fold_in(keys[6], part), 7)
    colloc = normal_values(part_splits[0], (BATCHES, PTS, L * BLK), 1.0, 6.0, ((0, 16),))
    blocks = draw_blocks(jax.random.fold_in(jax.random.fold_in(keys[6], part), 71), part)
    points = jnp.clip(jax.random.uniform(part_splits[2], (BATCHES, 3, PTS), jnp.float32, -3.0, 3.0) * levels(part_splits[2], (BATCHES, 3, PTS), ((0, 16),), -0.4, 0.0), -3.0, 3.0)
    centers = jnp.clip(jax.random.uniform(part_splits[3], (3, NBF), jnp.float32, -3.0, 3.0), -3.0, 3.0)
    exponents = jnp.clip(jnp.exp(jax.random.uniform(part_splits[4], (NBF,), jnp.float32, math.log(0.1), math.log(1.0))), 0.1, 1.0)
    density = normal_values(part_splits[5], (NBLK, BAND, BLK, BLK), ((L * BLK) ** -0.5), 0.3046875, ((0, 8),))
    return {"colloc": colloc, "blocks": blocks, "points": points, "centers": centers, "exponents": exponents, "density": density}


TABLE_RATES = (0.5, 2.0)
TABLE_WEIGHTS = (1.0, 0.5)


def exchange_terms(colloc, listed, points, centers, exponents, tile_set):
    listed_count = listed.shape[0]
    block_size = tile_set.shape[-1]
    full_width = listed_count * block_size
    density_sub = tile_set.transpose(0, 2, 1, 3).reshape(full_width, full_width)
    focused = jnp.dot(colloc, density_sub, preferred_element_type=jnp.float32).astype(jnp.bfloat16)
    centres = jnp.take(centers.reshape(3, -1, block_size), listed, axis=1).reshape(3, full_width)
    exponent_set = jnp.take(exponents.reshape(-1, block_size), listed, axis=0).reshape(full_width)
    offset_point = points[:, :, None] - centres[:, None, :]
    dist_point = jnp.sum(offset_point * offset_point, axis=0)
    across = centres[:, :, None] - centres[:, None, :]
    dist_pair = jnp.sum(across * across, axis=0)
    reduced = exponent_set[:, None] * exponent_set[None, :] / (exponent_set[:, None] + exponent_set[None, :])
    intersection = jnp.exp(-reduced * dist_pair).astype(jnp.bfloat16)
    potential = jnp.zeros(dist_point.shape, jnp.float32)
    for rate_k, weight_k in zip(TABLE_RATES, TABLE_WEIGHTS):
        screen = jnp.exp(-(exponent_set * rate_k / (exponent_set + rate_k))[None, :] * dist_point)
        scaled = (screen * focused.astype(jnp.float32)).astype(jnp.bfloat16)
        mixed_part = jnp.dot(scaled, intersection, preferred_element_type=jnp.float32)
        potential = potential + weight_k * screen * mixed_part
    field_bf = potential.astype(jnp.bfloat16)
    partial_k = jnp.dot(colloc.T, field_bf, preferred_element_type=jnp.float32).astype(jnp.bfloat16)
    return partial_k.reshape(listed_count, block_size, listed_count, block_size).transpose(0, 2, 1, 3)


def positions(block_ids):
    owners = N_BATCH * N_BLOCK
    return (block_ids % owners) * BLK_DEV + block_ids // owners


def reference(colloc, blocks, points, centers, exponents, density):
    band_width = density.shape[1]
    band_reach = band_width // 2
    stored = density.reshape(-1, BLK, BLK)
    classes = (jnp.arange(blocks.shape[0], dtype=jnp.int32) // BATCH_DEV) % N_REP

    def accumulate(running, batch_item):
        colloc_one, listed, points_one, replica = batch_item
        tile_index = positions(listed)[:, None] * band_width + (listed[None, :] - listed[:, None] + band_reach)
        tile_index = tile_index.astype(jnp.int32)
        tile_set = stored[tile_index]
        partial_k = exchange_terms(colloc_one, listed, points_one, centers, exponents, tile_set)
        running = running.at[replica, tile_index].add(partial_k.astype(jnp.float32))
        return running, None

    initial = jnp.zeros((N_REP, stored.shape[0], BLK, BLK), jnp.float32)
    totals = lax.scan(accumulate, initial, (colloc, blocks, points, classes))[0]
    rounded = lax.optimization_barrier(totals.astype(jnp.bfloat16)).astype(jnp.float32)
    return jnp.sum(rounded, axis=0).astype(jnp.bfloat16).reshape(density.shape)
```

```python
import functools

import jax
import jax.numpy as jnp
from jax import lax
from jax.experimental import pallas as pl
from jax.experimental.pallas import tpu as pltpu
from jax.sharding import PartitionSpec as P

TABLE_RATES = (0.5, 2.0)
TABLE_WEIGHTS = (1.0, 0.5)
MESH = pl.DeviceIdType.MESH
AXES = ("groups", "batch", "block", "rep")


def tables(blocks, owners, capacity, rows, band):
    batch_dev, listed_count = blocks.shape
    reach = band // 2
    flat = blocks.reshape(-1)
    count = flat.shape[0]
    target = flat % owners
    counter = jnp.arange(count, dtype=jnp.int32)
    before = (counter[:, None] > counter[None, :]) & (target[:, None] == target[None, :])
    ranking = jnp.sum(before.astype(jnp.int32), axis=1)
    slots = target * capacity + ranking
    offsets = (blocks[:, None, :] - blocks[:, :, None] + reach).reshape(count, listed_count)
    local = (flat // owners)[:, None] * band + offsets
    width = capacity * listed_count
    slot_axis = jnp.arange(owners * capacity, dtype=jnp.int32)
    taken = slot_axis[:, None] == slots[None, :]
    wanted = jnp.sum(jnp.where(taken[:, :, None], local[None], 0), axis=1).reshape(owners, width)
    entry = jnp.sum(jnp.where(taken, counter[None, :], 0), axis=1)
    owner_axis = jnp.arange(owners, dtype=jnp.int32)
    tile_axis = jnp.arange(rows * band, dtype=jnp.int32)
    place = ranking[:, None] * listed_count + jnp.arange(listed_count, dtype=jnp.int32)[None, :]
    hit = (target[None, None, :, None] == owner_axis[:, None, None, None]) & (
        local[None, None] == tile_axis[None, :, None, None]
    )
    where = width + jnp.sum(jnp.where(hit, place[None, None] - width, 0), axis=(2, 3))
    message = jnp.concatenate([wanted, where], axis=1)
    message = jnp.pad(message, ((0, 0), (0, 128 - message.shape[1])))
    message = jnp.broadcast_to(message[:, None, :], (owners, 8, 128))
    return jnp.concatenate([flat, slots * listed_count, entry]), message


def kernel(
    owners,
    n_block,
    capacity,
    table,
    message,
    colloc,
    points,
    functions,
    density,
    out,
    asked,
    asked_s,
    sending,
    arrived,
    parts,
    returned,
    classes,
    other,
    screens,
    overlap,
    flipped,
    gathered,
    field,
    ask_send,
    ask_recv,
    tile_send,
    tile_recv,
    back_send,
    back_recv,
    rep_send,
    rep_recv,
    local_sem,
):
    group = lax.axis_index("groups")
    rep = lax.axis_index("rep")
    me = lax.axis_index("batch") * n_block + lax.axis_index("block")
    batch_dev, pts, full = colloc.shape
    blk = density.shape[-1]
    listed = full // blk
    entries = batch_dev * listed
    width = capacity * listed
    tiles = density.shape[0]
    half = tiles // 2

    def device(s):
        return (group, s // n_block, s % n_block, rep)

    partner = (group, lax.axis_index("batch"), lax.axis_index("block"), 1 - rep)

    def peers(body):
        def step(k, carry):
            body(lax.rem(me + k, owners))
            return carry

        lax.fori_loop(1, owners, step, 0)

    barrier = pltpu.get_barrier_semaphore()
    peers(lambda s: pl.semaphore_signal(barrier, inc=1, device_id=device(s), device_id_type=MESH))
    pl.semaphore_signal(barrier, inc=1, device_id=partner, device_id_type=MESH)
    pl.semaphore_wait(barrier, owners)

    def remote(src, dst_at, dst, send, recv, s, slot):
        return pltpu.make_async_remote_copy(
            src_ref=src,
            dst_ref=dst.at[dst_at],
            send_sem=send.at[s],
            recv_sem=recv.at[slot],
            device_id=device(s),
            device_id_type=MESH,
        )

    def ask(s, slot):
        return remote(message.at[s], slot, asked, ask_send, ask_recv, s, slot)

    def serve(s, slot):
        return pltpu.make_async_remote_copy(
            src_ref=sending.at[s],
            dst_ref=arrived.at[pl.ds(slot * width, width)],
            send_sem=tile_send.at[s],
            recv_sem=tile_recv.at[slot],
            device_id=device(s),
            device_id_type=MESH,
        )

    def give(s, slot):
        return pltpu.make_async_remote_copy(
            src_ref=sending.at[s],
            dst_ref=returned.at[slot, pl.ds(0, width)],
            send_sem=back_send.at[s],
            recv_sem=back_recv.at[slot],
            device_id=device(s),
            device_id_type=MESH,
        )

    peers(lambda s: ask(s, me).start())
    own = pltpu.make_async_copy(message.at[me], asked.at[me], local_sem)
    own.start()
    own.wait()
    peers(lambda s: ask(s, s).wait_recv())
    to_scalar = pltpu.make_async_copy(asked, asked_s, local_sem)
    to_scalar.start()
    to_scalar.wait()

    def send_tiles(s):
        for t in range(width):
            sending[s, t] = density[asked_s[s, 0, t]]
        serve(s, me).start()

    peers(send_tiles)
    for t in range(width):
        arrived[me * width + t] = density[asked_s[me, 0, t]]

    def column(row):
        return jnp.broadcast_to(row, (blk, blk)).T

    def prepare(b, carry):
        rows = []
        for i in range(listed):
            block = functions[table[b * listed + i]]
            rows.append([block[k : k + 1] for k in range(4)])
        for i in range(listed):
            cols = [column(r) for r in rows[i]]
            for j in range(listed):
                dist = sum((cols[k] - rows[j][k]) * (cols[k] - rows[j][k]) for k in range(3))
                reduced = cols[3] * rows[j][3] / (cols[3] + rows[j][3])
                overlap[b, i * blk : (i + 1) * blk, j * blk : (j + 1) * blk] = jnp.exp(
                    -reduced * dist
                ).astype(jnp.bfloat16)
        rates = [
            [-(rows[j][3] * rate / (rows[j][3] + rate)) for rate in TABLE_RATES]
            for j in range(listed)
        ]

        def chunk(c, inner):
            lane = pl.ds(pl.multiple_of(c * blk, blk), blk)
            spot = [column(points[b, k : k + 1, lane]) for k in range(3)]
            for j in range(listed):
                dist = sum((spot[k] - rows[j][k]) * (spot[k] - rows[j][k]) for k in range(3))
                for n in range(len(TABLE_RATES)):
                    screens[b, n, lane, j * blk : (j + 1) * blk] = jnp.exp(rates[j][n] * dist)
            return inner

        lax.fori_loop(0, pts // blk, chunk, 0)
        flipped[b] = colloc[b].T
        return carry

    lax.fori_loop(0, batch_dev, prepare, 0)
    for s in range(owners):
        returned[s, width] = jnp.zeros((blk, blk), jnp.bfloat16)

    peers(lambda s: serve(s, s).wait_recv())

    def build(b, carry):
        for i in range(listed):
            slot = table[entries + b * listed + i]
            for j in range(listed):
                gathered[i * blk : (i + 1) * blk, j * blk : (j + 1) * blk] = arrived[
                    slot + j
                ]
        step = min(256, pts)
        for c in range(pts // step):
            span = slice(c * step, (c + 1) * step)
            focused = jnp.dot(
                colloc[b, span, :], gathered[...], preferred_element_type=jnp.float32
            ).astype(jnp.bfloat16).astype(jnp.float32)
            potential = None
            for n, weight in enumerate(TABLE_WEIGHTS):
                screen = screens[b, n, span, :]
                mixed = jnp.dot(
                    (screen * focused).astype(jnp.bfloat16),
                    overlap[b],
                    preferred_element_type=jnp.float32,
                )
                term = weight * screen * mixed
                potential = term if potential is None else potential + term
            field[span, :] = potential.astype(jnp.bfloat16)
        for i in range(listed):
            block = jnp.dot(
                flipped[b, i * blk : (i + 1) * blk, :],
                field[...],
                preferred_element_type=jnp.float32,
            ).astype(jnp.bfloat16)
            for j in range(listed):
                parts[b * listed + i, j] = block[:, j * blk : (j + 1) * blk]
        return carry

    lax.fori_loop(0, batch_dev, build, 0)

    def send_back(s):
        serve(s, me).wait_send()
        for k in range(capacity):
            entry = table[2 * entries + s * capacity + k]
            for j in range(listed):
                sending[s, k * listed + j] = parts[entry, j]
        give(s, me).start()

    peers(send_back)
    for k in range(capacity):
        entry = table[2 * entries + me * capacity + k]
        for j in range(listed):
            returned[me, k * listed + j] = parts[entry, j]
    peers(lambda s: give(s, s).wait_recv())

    def collect(r, carry):
        def add(s, total):
            return total + returned[s, asked_s[s, 0, width + r]].astype(jnp.float32)

        total = returned[0, asked_s[0, 0, width + r]].astype(jnp.float32)
        if owners <= 8:
            for s in range(1, owners):
                total = add(s, total)
        else:
            total = lax.fori_loop(1, owners, add, total)
        classes[r] = total.astype(jnp.bfloat16)
        return carry

    lax.fori_loop(0, tiles, collect, 0)

    swap = pltpu.make_async_remote_copy(
        src_ref=classes.at[pl.ds((1 - rep) * half, half)],
        dst_ref=other,
        send_sem=rep_send,
        recv_sem=rep_recv,
        device_id=partner,
        device_id_type=MESH,
    )
    swap.start()
    swap.wait()

    def finish(r, carry):
        out[r] = (
            classes[rep * half + r].astype(jnp.float32) + other[r].astype(jnp.float32)
        ).astype(jnp.bfloat16)
        return carry

    lax.fori_loop(0, half, finish, 0)
    peers(lambda s: ask(s, me).wait_send())
    peers(lambda s: give(s, me).wait_send())


def per_device(colloc, blocks, points, centers, exponents, density):
    n_block = lax.axis_size("block")
    owners = lax.axis_size("batch") * n_block
    batch_dev, listed = blocks.shape
    rows, band, blk, _ = density.shape
    pts, full = colloc.shape[1:]
    region = batch_dev * (band // 2 + 1)
    capacity = (region + owners - 1) // owners
    width = capacity * listed
    tiles = rows * band
    table, message = tables(blocks, owners, capacity, rows, band)
    functions = jnp.concatenate([centers, exponents[None, :]], axis=0)
    functions = functions.reshape(4, -1, blk).transpose(1, 0, 2)
    vmem = pl.BlockSpec(memory_space=pltpu.VMEM)
    bf16 = jnp.bfloat16
    result = pl.pallas_call(
        functools.partial(kernel, owners, n_block, capacity),
        out_shape=jax.ShapeDtypeStruct((tiles // 2, blk, blk), bf16),
        in_specs=[pl.BlockSpec(memory_space=pltpu.SMEM)] + [vmem] * 5,
        out_specs=vmem,
        scratch_shapes=[
            pltpu.VMEM((owners, 8, 128), jnp.int32),
            pltpu.SMEM((owners, 8, 128), jnp.int32),
            pltpu.VMEM((owners, width, blk, blk), bf16),
            pltpu.VMEM((owners * width, blk, blk), bf16),
            pltpu.VMEM((batch_dev * listed, listed, blk, blk), bf16),
            pltpu.VMEM((owners, width + 1, blk, blk), bf16),
            pltpu.VMEM((tiles, blk, blk), bf16),
            pltpu.VMEM((tiles // 2, blk, blk), bf16),
            pltpu.VMEM((batch_dev, len(TABLE_RATES), pts, full), jnp.float32),
            pltpu.VMEM((batch_dev, full, full), bf16),
            pltpu.VMEM((batch_dev, full, pts), bf16),
            pltpu.VMEM((full, full), bf16),
            pltpu.VMEM((pts, full), bf16),
            pltpu.SemaphoreType.DMA((owners,)),
            pltpu.SemaphoreType.DMA((owners,)),
            pltpu.SemaphoreType.DMA((owners,)),
            pltpu.SemaphoreType.DMA((owners,)),
            pltpu.SemaphoreType.DMA((owners,)),
            pltpu.SemaphoreType.DMA((owners,)),
            pltpu.SemaphoreType.DMA,
            pltpu.SemaphoreType.DMA,
            pltpu.SemaphoreType.DMA,
        ],
        compiler_params=pltpu.CompilerParams(
            collective_id=0, has_side_effects=True, vmem_limit_bytes=56 * 1024 * 1024
        ),
    )(
        table,
        message,
        colloc,
        points,
        functions,
        density.reshape(tiles, blk, blk),
    )
    return result.reshape(rows // 2, band, blk, blk)


def solution(mesh):
    in_specs = (
        P(AXES, None, None),
        P(AXES, None),
        P(AXES, None, None),
        P(None, "groups"),
        P("groups"),
        P(("groups", "batch", "block"), None, None, None),
    )
    out_specs = P(AXES, None, None, None)
    return jax.shard_map(
        per_device, mesh=mesh, in_specs=in_specs, out_specs=out_specs, check_vma=False
    )
```

```python
import functools

import jax
import jax.numpy as jnp
from jax import lax
from jax.experimental import pallas as pl
from jax.experimental.pallas import tpu as pltpu
from jax.sharding import PartitionSpec as P

TABLE_RATES = (0.5, 2.0)
TABLE_WEIGHTS = (1.0, 0.5)
MESH = pl.DeviceIdType.MESH
AXES = ("groups", "batch", "block", "rep")


def tables(blocks, owners, capacity, rows, band, reps):
    batch_dev, listed_count = blocks.shape
    reach = band // 2
    flat = blocks.reshape(-1)
    count = flat.shape[0]
    target = flat % owners
    counter = jnp.arange(count, dtype=jnp.int32)
    before = (counter[:, None] > counter[None, :]) & (target[:, None] == target[None, :])
    ranking = jnp.sum(before.astype(jnp.int32), axis=1)
    slots = target * capacity + ranking
    offsets = (blocks[:, None, :] - blocks[:, :, None] + reach).reshape(count, listed_count)
    local = (flat // owners)[:, None] * band + offsets
    width = capacity * listed_count
    chips = owners // 2
    slot_axis = jnp.arange(owners * capacity, dtype=jnp.int32)
    taken = slot_axis[:, None] == slots[None, :]
    wanted = jnp.sum(jnp.where(taken[:, :, None], local[None], 0), axis=1).reshape(owners, width)
    entry = jnp.sum(jnp.where(taken, counter[None, :], 0), axis=1)
    owner_axis = jnp.arange(owners, dtype=jnp.int32)
    tile_axis = jnp.arange(rows * band, dtype=jnp.int32)
    place = ranking[:, None] * listed_count + jnp.arange(listed_count, dtype=jnp.int32)[None, :]
    hit = (target[None, None, :, None] == owner_axis[:, None, None, None]) & (
        local[None, None] == tile_axis[None, :, None, None]
    )
    where = width + jnp.sum(jnp.where(hit, place[None, None] - width, 0), axis=(2, 3))
    message = jnp.concatenate([wanted, where], axis=1)
    message = message.reshape(2, chips, -1).transpose(1, 0, 2)
    message = jnp.pad(message, ((0, 0), (0, 6), (0, 128 - message.shape[2])))
    base = ((target % chips) * (2 * reps) + target // chips) * width + ranking * listed_count
    return jnp.concatenate([flat, base, entry]), message


def kernel(
    n_batch,
    n_block,
    reps,
    capacity,
    table,
    message,
    colloc,
    points,
    centers,
    exponents,
    density,
    out,
    asked,
    asked_s,
    functions,
    spots,
    mine,
    mirror,
    sending,
    arrived,
    parts,
    returned_side,
    returned_far,
    sums,
    sums_own,
    sums_mirror,
    rest,
    other,
    screens,
    overlap,
    flipped,
    gathered,
    field,
    ask_send,
    ask_recv,
    tile_send,
    tile_recv,
    back_send,
    back_recv,
    single,
    local_sem,
):
    group = lax.axis_index("groups")
    row = lax.axis_index("batch")
    col = lax.axis_index("block")
    rep = lax.axis_index("rep")
    depth = n_batch // 2
    side = row // depth
    far = 1 - side
    count = depth * n_block * reps
    me = ((row % depth) * n_block + col) * reps + rep
    batch_dev, pts, full = colloc.shape
    tiles, part, blk = mine.shape
    listed = full // blk
    entries = batch_dev * listed
    width = capacity * listed
    kept = tiles // reps
    mine_rows = pl.ds(pl.multiple_of(rep * part, part), part)
    bf16 = jnp.bfloat16

    def device(p):
        chip = p // reps
        return (group, side * depth + chip // n_block, chip % n_block, p % reps)

    across = (group, far * depth + row % depth, col, rep)
    partner = (group, row, col, 1 - rep)

    def peers(body):
        def step(k, carry):
            body(lax.rem(me + k, count))
            return carry

        lax.fori_loop(1, count, step, 0)

    load = pltpu.make_async_copy(density.at[:, mine_rows], mine, local_sem)
    load.start()
    barrier = pltpu.get_barrier_semaphore()
    peers(lambda p: pl.semaphore_signal(barrier, inc=1, device_id=device(p), device_id_type=MESH))
    pl.semaphore_signal(barrier, inc=1, device_id=across, device_id_type=MESH)
    pl.semaphore_wait(barrier, count)
    load.wait()

    def send(src, dst, out_sem, in_sem, where):
        return pltpu.make_async_remote_copy(
            src_ref=src,
            dst_ref=dst,
            send_sem=out_sem,
            recv_sem=in_sem,
            device_id=where,
            device_id_type=MESH,
        )

    def ask(p, slot):
        return send(
            message.at[p // reps], asked.at[slot], ask_send.at[p], ask_recv.at[slot], device(p)
        )

    def serve(p, slot, h):
        return send(
            sending.at[p, h],
            arrived.at[pl.ds((slot * 2 + h) * width, width)],
            tile_send.at[p, h],
            tile_recv.at[slot, h],
            device(p),
        )

    def give(p, slot, h, returned):
        return send(
            sending.at[p, h],
            returned.at[slot, pl.ds(0, width)],
            back_send.at[p, h],
            back_recv.at[slot, h],
            device(p),
        )

    peers(lambda p: ask(p, me).start())
    swap_in = send(mine, mirror, single.at[0], single.at[1], across)
    swap_in.start()
    own = pltpu.make_async_copy(message.at[me // reps], asked.at[me], local_sem)
    own.start()
    own.wait()
    peers(lambda p: ask(p, p).wait_recv())
    to_scalar = pltpu.make_async_copy(asked, asked_s, local_sem)
    to_scalar.start()
    to_scalar.wait()

    def send_tiles(source, h):
        def one(p):
            for t in range(width):
                sending[p, h, t] = source[asked_s[p, h, t]]
            serve(p, me, h).start()

        peers(one)
        for t in range(width):
            arrived[(me * 2 + h) * width + t] = source[asked_s[me, h, t]]

    send_tiles(mine, side)

    def arrange(l, carry):
        lane = pl.ds(pl.multiple_of(l * blk, blk), blk)
        for k in range(3):
            functions[l, k : k + 1] = centers[k : k + 1, lane]
        functions[l, 3:4] = exponents[0:1, lane]
        return carry

    lax.fori_loop(0, functions.shape[0], arrange, 0)
    for b in range(batch_dev):
        for k in range(3):
            spots[b, k : k + 1] = points[k, b : b + 1]

    def column(line):
        return jnp.broadcast_to(line, (blk, blk)).T

    def prepare(b, carry):
        rows = []
        for i in range(listed):
            block = functions[table[b * listed + i]]
            rows.append([block[k : k + 1] for k in range(4)])
        for i in range(listed):
            cols = [column(r) for r in rows[i]]
            for j in range(listed):
                dist = sum((cols[k] - rows[j][k]) * (cols[k] - rows[j][k]) for k in range(3))
                reduced = cols[3] * rows[j][3] / (cols[3] + rows[j][3])
                overlap[b, i * blk : (i + 1) * blk, j * blk : (j + 1) * blk] = jnp.exp(
                    -reduced * dist
                ).astype(bf16)
        rates = [
            [-(rows[j][3] * rate / (rows[j][3] + rate)) for rate in TABLE_RATES]
            for j in range(listed)
        ]

        def chunk(c, inner):
            lane = pl.ds(pl.multiple_of(c * blk, blk), blk)
            spot = [column(spots[b, k : k + 1, lane]) for k in range(3)]
            for j in range(listed):
                dist = sum((spot[k] - rows[j][k]) * (spot[k] - rows[j][k]) for k in range(3))
                for n in range(len(TABLE_RATES)):
                    screens[b, n, lane, j * blk : (j + 1) * blk] = jnp.exp(rates[j][n] * dist)
            return inner

        lax.fori_loop(0, pts // blk, chunk, 0)
        flipped[b] = colloc[b].T
        return carry

    lax.fori_loop(0, batch_dev, prepare, 0)

    def blank(p, carry):
        returned_side[p, width] = jnp.zeros((part, blk), bf16)
        returned_far[p, width] = jnp.zeros((part, blk), bf16)
        return carry

    lax.fori_loop(0, count, blank, 0)

    swap_in.wait_recv()
    send_tiles(mirror, far)
    peers(lambda p: serve(p, p, side).wait_recv())
    peers(lambda p: serve(p, p, far).wait_recv())

    def build(b, carry):
        for i in range(listed):
            slot = table[entries + b * listed + i]
            for j in range(listed):
                for c in range(reps):
                    top = i * blk + c * part
                    gathered[top : top + part, j * blk : (j + 1) * blk] = arrived[
                        slot + (2 * width * c + j)
                    ]
        step = min(256, pts)
        for c in range(pts // step):
            span = slice(c * step, (c + 1) * step)
            focused = (
                jnp.dot(colloc[b, span, :], gathered[...], preferred_element_type=jnp.float32)
                .astype(bf16)
                .astype(jnp.float32)
            )
            potential = None
            for n, weight in enumerate(TABLE_WEIGHTS):
                screen = screens[b, n, span, :]
                mixed = jnp.dot(
                    (screen * focused).astype(bf16), overlap[b], preferred_element_type=jnp.float32
                )
                term = weight * screen * mixed
                potential = term if potential is None else potential + term
            field[span, :] = potential.astype(bf16)
        for i in range(listed):
            block = jnp.dot(
                flipped[b, i * blk : (i + 1) * blk, :],
                field[...],
                preferred_element_type=jnp.float32,
            ).astype(bf16)
            for j in range(listed):
                for c in range(reps):
                    parts[((b * listed + i) * listed + j) * reps + c] = block[
                        c * part : (c + 1) * part, j * blk : (j + 1) * blk
                    ]
        return carry

    lax.fori_loop(0, batch_dev, build, 0)

    def send_back(h, returned):
        first = 2 * entries + h * (count // reps) * capacity

        def one(p):
            serve(p, me, h).wait_send()
            for k in range(capacity):
                entry = table[first + (p // reps) * capacity + k]
                for j in range(listed):
                    sending[p, h, k * listed + j] = parts[
                        entry * (listed * reps) + (j * reps + p % reps)
                    ]
            give(p, me, h, returned).start()

        peers(one)
        for k in range(capacity):
            entry = table[first + (me // reps) * capacity + k]
            for j in range(listed):
                returned[me, k * listed + j] = parts[
                    entry * (listed * reps) + (j * reps + rep)
                ]

    def total(r, h, returned):
        def add(p, running):
            return running + returned[p, asked_s[p, h, width + r]].astype(jnp.float32)

        running = jnp.zeros((part, blk), jnp.float32)
        if count <= 8:
            for p in range(count):
                running = add(p, running)
            return running
        return lax.fori_loop(0, count, add, running)

    send_back(far, returned_far)
    send_back(side, returned_side)
    peers(lambda p: give(p, p, far, returned_far).wait_recv())

    def collect_far(r, carry):
        sums[r] = total(r, far, returned_far).astype(bf16)
        return carry

    lax.fori_loop(0, tiles, collect_far, 0)
    swap_out = send(sums, sums_mirror, single.at[2], single.at[3], across)
    swap_out.start()
    peers(lambda p: give(p, p, side, returned_side).wait_recv())

    def collect_own(r, carry):
        sums_own[r] = total(r, side, returned_side)
        return carry

    lax.fori_loop(0, tiles, collect_own, 0)
    swap_out.wait_recv()

    def combine(first, r):
        return (sums_own[first + r] + sums_mirror[first + r].astype(jnp.float32)).astype(bf16)

    def pass_on(r, carry):
        rest[r] = combine((1 - rep) * kept, r)
        return carry

    lax.fori_loop(0, kept, pass_on, 0)
    hand = send(rest, other, single.at[4], single.at[5], partner)
    hand.start()

    def keep(r, carry):
        out[r, mine_rows] = combine(rep * kept, r)
        return carry

    lax.fori_loop(0, kept, keep, 0)
    hand.wait_recv()

    other_rows = pl.ds(pl.multiple_of((1 - rep) * part, part), part)

    def finish(r, carry):
        out[r, other_rows] = other[r]
        return carry

    lax.fori_loop(0, kept, finish, 0)
    hand.wait_send()
    swap_in.wait_send()
    swap_out.wait_send()
    peers(lambda p: ask(p, me).wait_send())
    peers(lambda p: give(p, me, side, returned_side).wait_send())
    peers(lambda p: give(p, me, far, returned_far).wait_send())


def per_device(colloc, blocks, points, centers, exponents, density):
    n_batch, n_block, reps = (lax.axis_size(name) for name in AXES[1:])
    owners = n_batch * n_block
    batch_dev, listed = blocks.shape
    rows, band, blk, _ = density.shape
    pts, full = colloc.shape[1:]
    region = batch_dev * (band // 2 + 1)
    capacity = (region + owners - 1) // owners
    width = capacity * listed
    tiles = rows * band
    count = owners // 2 * reps
    part = blk // reps
    table, message = tables(blocks, owners, capacity, rows, band, reps)
    vmem = pl.BlockSpec(memory_space=pltpu.VMEM)
    bf16 = jnp.bfloat16
    result = pl.pallas_call(
        functools.partial(kernel, n_batch, n_block, reps, capacity),
        out_shape=jax.ShapeDtypeStruct((tiles // reps, blk, blk), bf16),
        in_specs=[pl.BlockSpec(memory_space=pltpu.SMEM)]
        + [vmem] * 5
        + [pl.BlockSpec(memory_space=pl.ANY)],
        out_specs=vmem,
        scratch_shapes=[
            pltpu.VMEM((count, 8, 128), jnp.int32),
            pltpu.SMEM((count, 8, 128), jnp.int32),
            pltpu.VMEM((centers.shape[1] // blk, 4, blk), jnp.float32),
            pltpu.VMEM((batch_dev, 3, pts), jnp.float32),
            pltpu.VMEM((tiles, part, blk), bf16),
            pltpu.VMEM((tiles, part, blk), bf16),
            pltpu.VMEM((count, 2, width, part, blk), bf16),
            pltpu.VMEM((count * 2 * width, part, blk), bf16),
            pltpu.VMEM((batch_dev * listed * listed * reps, part, blk), bf16),
            pltpu.VMEM((count, width + 1, part, blk), bf16),
            pltpu.VMEM((count, width + 1, part, blk), bf16),
            pltpu.VMEM((tiles, part, blk), bf16),
            pltpu.VMEM((tiles, part, blk), jnp.float32),
            pltpu.VMEM((tiles, part, blk), bf16),
            pltpu.VMEM((tiles // reps, part, blk), bf16),
            pltpu.VMEM((tiles // reps, part, blk), bf16),
            pltpu.VMEM((batch_dev, len(TABLE_RATES), pts, full), jnp.float32),
            pltpu.VMEM((batch_dev, full, full), bf16),
            pltpu.VMEM((batch_dev, full, pts), bf16),
            pltpu.VMEM((full, full), bf16),
            pltpu.VMEM((pts, full), bf16),
            pltpu.SemaphoreType.DMA((count,)),
            pltpu.SemaphoreType.DMA((count,)),
            pltpu.SemaphoreType.DMA((count, 2)),
            pltpu.SemaphoreType.DMA((count, 2)),
            pltpu.SemaphoreType.DMA((count, 2)),
            pltpu.SemaphoreType.DMA((count, 2)),
            pltpu.SemaphoreType.DMA((6,)),
            pltpu.SemaphoreType.DMA,
        ],
        compiler_params=pltpu.CompilerParams(
            collective_id=0, has_side_effects=True, vmem_limit_bytes=56 * 1024 * 1024
        ),
    )(
        table,
        message,
        colloc,
        points.transpose(1, 0, 2),
        centers,
        exponents.reshape(1, -1),
        density.reshape(tiles, blk, blk),
    )
    return result.reshape(rows // reps, band, blk, blk)


def solution(mesh):
    in_specs = (
        P(AXES, None, None),
        P(AXES, None),
        P(AXES, None, None),
        P(None, "groups"),
        P("groups"),
        P(("groups", "batch", "block"), None, None, None),
    )
    out_specs = P(AXES, None, None, None)
    return jax.shard_map(
        per_device, mesh=mesh, in_specs=in_specs, out_specs=out_specs, check_vma=False
    )
```

```python
import functools

import jax
import jax.numpy as jnp
from jax import lax
from jax.experimental import pallas as pl
from jax.experimental.pallas import tpu as pltpu
from jax.sharding import PartitionSpec as P

TABLE_RATES = (0.5, 2.0)
TABLE_WEIGHTS = (1.0, 0.5)
MESH = pl.DeviceIdType.MESH
CHUNKS = 2
AXES = ("groups", "batch", "block", "rep")


def tables(blocks, owners, capacity, rows, band, reps):
    batch_dev, listed_count = blocks.shape
    reach = band // 2
    flat = blocks.reshape(-1)
    count = flat.shape[0]
    target = flat % owners
    counter = jnp.arange(count, dtype=jnp.int32)
    before = (counter[:, None] > counter[None, :]) & (target[:, None] == target[None, :])
    ranking = jnp.sum(before.astype(jnp.int32), axis=1)
    slots = target * capacity + ranking
    offsets = (blocks[:, None, :] - blocks[:, :, None] + reach).reshape(count, listed_count)
    local = (flat // owners)[:, None] * band + offsets
    width = capacity * listed_count
    chips = owners // 2
    slot_axis = jnp.arange(owners * capacity, dtype=jnp.int32)
    taken = slot_axis[:, None] == slots[None, :]
    wanted = jnp.sum(jnp.where(taken[:, :, None], local[None], 0), axis=1).reshape(owners, width)
    entry = jnp.sum(jnp.where(taken, counter[None, :], 0), axis=1)
    owner_axis = jnp.arange(owners, dtype=jnp.int32)
    tile_axis = jnp.arange(rows * band, dtype=jnp.int32)
    place = ranking[:, None] * listed_count + jnp.arange(listed_count, dtype=jnp.int32)[None, :]
    hit = (target[None, None, :, None] == owner_axis[:, None, None, None]) & (
        local[None, None] == tile_axis[None, :, None, None]
    )
    where = width + jnp.sum(jnp.where(hit, place[None, None] - width, 0), axis=(2, 3))
    message = jnp.concatenate([wanted, where], axis=1)
    message = message.reshape(2, chips, -1).transpose(1, 0, 2)
    message = jnp.pad(message, ((0, 0), (0, 6), (0, 128 - message.shape[2])))
    base = ((target % chips) * (2 * reps) + target // chips) * width + ranking * listed_count
    return jnp.concatenate([flat, base, entry]), message


def kernel(
    n_batch,
    n_block,
    reps,
    capacity,
    table,
    message,
    colloc,
    points,
    centers,
    exponents,
    density,
    out,
    asked,
    asked_s,
    functions,
    spots,
    mine,
    mirror,
    sending_side,
    sending_far,
    arrived,
    parts,
    returned_side,
    returned_far,
    sums,
    sums_own,
    far_in,
    rest,
    other,
    screens,
    overlap,
    flipped,
    gathered,
    field,
    colloc_v,
    ask_send,
    ask_recv,
    tile_send,
    tile_recv,
    back_send,
    back_recv,
    swap_send,
    swap_recv,
    out_send,
    out_recv,
    hand_send,
    hand_recv,
    colloc_sem,
    local_sem,
):
    group = lax.axis_index("groups")
    row = lax.axis_index("batch")
    col = lax.axis_index("block")
    rep = lax.axis_index("rep")
    depth = n_batch // 2
    side = row // depth
    far = 1 - side
    count = depth * n_block * reps
    me = ((row % depth) * n_block + col) * reps + rep
    batch_dev, pts, full = colloc.shape
    tiles, part, blk = mine.shape
    sub = part // CHUNKS
    listed = full // blk
    entries = batch_dev * listed
    width = capacity * listed
    kept = tiles // reps
    mine_rows = pl.ds(pl.multiple_of(rep * part, part), part)
    bf16 = jnp.bfloat16

    def device(p):
        chip = p // reps
        return (group, side * depth + chip // n_block, chip % n_block, p % reps)

    def across(c):
        return (group, far * depth + row % depth, col, c)

    partner = (group, row, col, 1 - rep)

    def peers(body):
        def step(k, carry):
            body(lax.rem(me + k, count))
            return carry

        lax.fori_loop(1, count, step, 0)

    load = pltpu.make_async_copy(density.at[:, mine_rows], mine, local_sem)
    load.start()
    load_colloc = pltpu.make_async_copy(colloc, colloc_v, colloc_sem)
    load_colloc.start()
    barrier = pltpu.get_barrier_semaphore()
    peers(lambda p: pl.semaphore_signal(barrier, inc=1, device_id=device(p), device_id_type=MESH))
    for c in range(reps):
        pl.semaphore_signal(barrier, inc=1, device_id=across(c), device_id_type=MESH)
    pl.semaphore_wait(barrier, count - 1 + reps)
    load.wait()

    def send(src, dst, out_sem, in_sem, where):
        return pltpu.make_async_remote_copy(
            src_ref=src,
            dst_ref=dst,
            send_sem=out_sem,
            recv_sem=in_sem,
            device_id=where,
            device_id_type=MESH,
        )

    def ask(p, slot):
        return send(
            message.at[p // reps], asked.at[slot], ask_send.at[p], ask_recv.at[slot], device(p)
        )

    def packed(p, q):
        return sending_side.at[p] if q is None else sending_far.at[q, p]

    def mark(q):
        return 0 if q is None else 1 + q

    def span_of(q):
        return slice(0, part) if q is None else slice(q * sub, (q + 1) * sub)

    def serve(p, slot, q):
        first = (slot * 2 + (side if q is None else far)) * width
        span = span_of(q)
        return send(
            packed(p, q),
            arrived.at[pl.ds(first, width), pl.ds(span.start, span.stop - span.start)],
            tile_send.at[p, mark(q)],
            tile_recv.at[slot, mark(q)],
            device(p),
        )

    def give(p, slot, q):
        landing = returned_side if q is None else returned_far[q]
        return send(
            packed(p, q),
            landing.at[slot, pl.ds(0, width)],
            back_send.at[p, mark(q)],
            back_recv.at[slot, mark(q)],
            device(p),
        )

    def swap_in(q):
        return send(
            mine.at[:, pl.ds(q * sub, sub)],
            mirror[q],
            swap_send.at[q],
            swap_recv.at[q],
            across(rep),
        )

    def swap_out(q, c, source):
        return send(
            sums[q].at[pl.ds(c * kept, kept)],
            far_in.at[source, :, pl.ds(q * sub, sub)],
            out_send.at[q, c],
            out_recv.at[q, source],
            across(c),
        )

    peers(lambda p: ask(p, me).start())
    swap_in(0).start()
    own = pltpu.make_async_copy(message.at[me // reps], asked.at[me], local_sem)
    own.start()
    own.wait()
    peers(lambda p: ask(p, p).wait_recv())
    to_scalar = pltpu.make_async_copy(asked, asked_s, local_sem)
    to_scalar.start()
    to_scalar.wait()

    def send_tiles(q):
        h = side if q is None else far
        source = mine if q is None else mirror[q]
        span = span_of(q)

        def one(p):
            target = packed(p, q)
            for t in range(width):
                target[t] = source[asked_s[p, h, t]]
            serve(p, me, q).start()

        peers(one)
        for t in range(width):
            arrived[(me * 2 + h) * width + t, span] = source[asked_s[me, h, t]]

    send_tiles(None)

    def arrange(l, carry):
        lane = pl.ds(pl.multiple_of(l * blk, blk), blk)
        for k in range(3):
            functions[l, k : k + 1] = centers[k : k + 1, lane]
        functions[l, 3:4] = exponents[0:1, lane]
        return carry

    lax.fori_loop(0, functions.shape[0], arrange, 0)
    for b in range(batch_dev):
        for k in range(3):
            spots[b, k : k + 1] = points[k, b : b + 1]

    def column(line):
        return jnp.broadcast_to(line, (blk, blk)).T

    def prepare(b, carry):
        rows = []
        for i in range(listed):
            block = functions[table[b * listed + i]]
            rows.append([block[k : k + 1] for k in range(4)])
        for i in range(listed):
            cols = [column(r) for r in rows[i]]
            for j in range(listed):
                dist = sum((cols[k] - rows[j][k]) * (cols[k] - rows[j][k]) for k in range(3))
                reduced = cols[3] * rows[j][3] / (cols[3] + rows[j][3])
                overlap[b, i * blk : (i + 1) * blk, j * blk : (j + 1) * blk] = jnp.exp(
                    -reduced * dist
                ).astype(bf16)
        rates = [
            [-(rows[j][3] * rate / (rows[j][3] + rate)) for rate in TABLE_RATES]
            for j in range(listed)
        ]

        def chunk(c, inner):
            lane = pl.ds(pl.multiple_of(c * blk, blk), blk)
            spot = [column(spots[b, k : k + 1, lane]) for k in range(3)]
            for j in range(listed):
                dist = sum((spot[k] - rows[j][k]) * (spot[k] - rows[j][k]) for k in range(3))
                for n in range(len(TABLE_RATES)):
                    screens[b, n, lane, j * blk : (j + 1) * blk] = jnp.exp(rates[j][n] * dist)
            return inner

        lax.fori_loop(0, pts // blk, chunk, 0)
        flipped[b] = colloc_v[b].T
        return carry

    load_colloc.wait()
    lax.fori_loop(0, batch_dev, prepare, 0)

    def blank(p, carry):
        returned_side[p, width] = jnp.zeros((part, blk), bf16)
        for q in range(CHUNKS):
            returned_far[q][p, width] = jnp.zeros((sub, blk), bf16)
        return carry

    lax.fori_loop(0, count, blank, 0)

    for q in range(CHUNKS):
        swap_in(q).wait_send()
        if q + 1 < CHUNKS:
            swap_in(q + 1).start()
        swap_in(q).wait_recv()
        send_tiles(q)
    for q in [None, *range(CHUNKS)]:
        peers(lambda p: serve(p, p, q).wait_recv())

    def build(b, carry):
        for i in range(listed):
            slot = table[entries + b * listed + i]
            for j in range(listed):
                for c in range(reps):
                    top = i * blk + c * part
                    gathered[top : top + part, j * blk : (j + 1) * blk] = arrived[
                        slot + (2 * width * c + j)
                    ]
        step = min(256, pts)
        for c in range(pts // step):
            span = slice(c * step, (c + 1) * step)
            focused = (
                jnp.dot(colloc_v[b, span, :], gathered[...], preferred_element_type=jnp.float32)
                .astype(bf16)
                .astype(jnp.float32)
            )
            potential = None
            for n, weight in enumerate(TABLE_WEIGHTS):
                screen = screens[b, n, span, :]
                mixed = jnp.dot(
                    (screen * focused).astype(bf16), overlap[b], preferred_element_type=jnp.float32
                )
                term = weight * screen * mixed
                potential = term if potential is None else potential + term
            field[span, :] = potential.astype(bf16)
        for i in range(listed):
            block = jnp.dot(
                flipped[b, i * blk : (i + 1) * blk, :],
                field[...],
                preferred_element_type=jnp.float32,
            ).astype(bf16)
            for j in range(listed):
                for c in range(reps):
                    parts[((b * listed + i) * listed + j) * reps + c] = block[
                        c * part : (c + 1) * part, j * blk : (j + 1) * blk
                    ]
        return carry

    lax.fori_loop(0, batch_dev, build, 0)

    def send_back(q):
        h = side if q is None else far
        first = 2 * entries + h * (count // reps) * capacity
        landing = returned_side if q is None else returned_far[q]
        span = span_of(q)

        def piece(p, k, j):
            entry = table[first + (p // reps) * capacity + k]
            return parts[entry * (listed * reps) + (j * reps + p % reps)][span]

        def one(p):
            serve(p, me, q).wait_send()
            target = packed(p, q)
            for k in range(capacity):
                for j in range(listed):
                    target[k * listed + j] = piece(p, k, j)
            give(p, me, q).start()

        peers(one)
        for k in range(capacity):
            for j in range(listed):
                landing[me, k * listed + j] = piece(me, k, j)

    def total(r, q):
        h = side if q is None else far
        landing = returned_side if q is None else returned_far[q]

        def add(p, running):
            return running + landing[p, asked_s[p, h, width + r]].astype(jnp.float32)

        if count <= 8:
            running = add(0, 0.0)
            for p in range(1, count):
                running = add(p, running)
            return running
        return lax.fori_loop(0, count, add, jnp.zeros(landing.shape[2:], jnp.float32))

    send_back(0)
    for q in range(CHUNKS):
        peers(lambda p: give(p, me, q).wait_send())
        send_back(q + 1 if q + 1 < CHUNKS else None)
        peers(lambda p: give(p, p, q).wait_recv())

        def collect_far(r, carry):
            sums[q][r] = total(r, q).astype(bf16)
            return carry

        lax.fori_loop(0, tiles, collect_far, 0)
        for c in range(reps):
            swap_out(q, c, rep).start()

    peers(lambda p: give(p, p, None).wait_recv())

    def pass_on(r, carry):
        rest[r] = total((1 - rep) * kept + r, None).astype(bf16)
        return carry

    lax.fori_loop(0, kept, pass_on, 0)
    hand = send(rest, other, hand_send, hand_recv, partner)
    hand.start()

    def collect_own(r, carry):
        sums_own[r] = total(rep * kept + r, None)
        return carry

    lax.fori_loop(0, kept, collect_own, 0)
    hand.wait_recv()
    for q in range(CHUNKS):
        for c in range(reps):
            swap_out(q, c, c).wait_recv()
    other_rows = pl.ds(pl.multiple_of((1 - rep) * part, part), part)

    def finish(r, carry):
        out[r, mine_rows] = (sums_own[r] + far_in[rep, r].astype(jnp.float32)).astype(bf16)
        out[r, other_rows] = (
            other[r].astype(jnp.float32) + far_in[1 - rep, r].astype(jnp.float32)
        ).astype(bf16)
        return carry

    lax.fori_loop(0, kept, finish, 0)
    hand.wait_send()
    for q in range(CHUNKS):
        for c in range(reps):
            swap_out(q, c, rep).wait_send()
    peers(lambda p: ask(p, me).wait_send())
    peers(lambda p: give(p, me, None).wait_send())


def per_device(colloc, blocks, points, centers, exponents, density):
    n_batch, n_block, reps = (lax.axis_size(name) for name in AXES[1:])
    owners = n_batch * n_block
    batch_dev, listed = blocks.shape
    rows, band, blk, _ = density.shape
    pts, full = colloc.shape[1:]
    region = batch_dev * (band // 2 + 1)
    capacity = (region + owners - 1) // owners
    width = capacity * listed
    tiles = rows * band
    count = owners // 2 * reps
    part = blk // reps
    sub = part // CHUNKS
    kept = tiles // reps
    table, message = tables(blocks, owners, capacity, rows, band, reps)
    vmem = pl.BlockSpec(memory_space=pltpu.VMEM)
    bf16 = jnp.bfloat16
    result = pl.pallas_call(
        functools.partial(kernel, n_batch, n_block, reps, capacity),
        out_shape=jax.ShapeDtypeStruct((tiles // reps, blk, blk), bf16),
        in_specs=[pl.BlockSpec(memory_space=pltpu.SMEM)]
        + [vmem, pl.BlockSpec(memory_space=pl.ANY)]
        + [vmem] * 3
        + [pl.BlockSpec(memory_space=pl.ANY)],
        out_specs=vmem,
        scratch_shapes=[
            pltpu.VMEM((count, 8, 128), jnp.int32),
            pltpu.SMEM((count, 8, 128), jnp.int32),
            pltpu.VMEM((centers.shape[1] // blk, 4, blk), jnp.float32),
            pltpu.VMEM((batch_dev, 3, pts), jnp.float32),
            pltpu.VMEM((tiles, part, blk), bf16),
            tuple(pltpu.VMEM((tiles, sub, blk), bf16) for _ in range(CHUNKS)),
            pltpu.VMEM((count, width, part, blk), bf16),
            pltpu.VMEM((CHUNKS, count, width, sub, blk), bf16),
            pltpu.VMEM((count * 2 * width, part, blk), bf16),
            pltpu.VMEM((batch_dev * listed * listed * reps, part, blk), bf16),
            pltpu.VMEM((count, width + 1, part, blk), bf16),
            tuple(pltpu.VMEM((count, width + 1, sub, blk), bf16) for _ in range(CHUNKS)),
            tuple(pltpu.VMEM((tiles, sub, blk), bf16) for _ in range(CHUNKS)),
            pltpu.VMEM((kept, part, blk), jnp.float32),
            pltpu.VMEM((reps, kept, part, blk), bf16),
            pltpu.VMEM((kept, part, blk), bf16),
            pltpu.VMEM((kept, part, blk), bf16),
            pltpu.VMEM((batch_dev, len(TABLE_RATES), pts, full), jnp.float32),
            pltpu.VMEM((batch_dev, full, full), bf16),
            pltpu.VMEM((batch_dev, full, pts), bf16),
            pltpu.VMEM((full, full), bf16),
            pltpu.VMEM((pts, full), bf16),
            pltpu.VMEM(colloc.shape, bf16),
            pltpu.SemaphoreType.DMA((count,)),
            pltpu.SemaphoreType.DMA((count,)),
            pltpu.SemaphoreType.DMA((count, 1 + CHUNKS)),
            pltpu.SemaphoreType.DMA((count, 1 + CHUNKS)),
            pltpu.SemaphoreType.DMA((count, 1 + CHUNKS)),
            pltpu.SemaphoreType.DMA((count, 1 + CHUNKS)),
            pltpu.SemaphoreType.DMA((CHUNKS,)),
            pltpu.SemaphoreType.DMA((CHUNKS,)),
            pltpu.SemaphoreType.DMA((CHUNKS, reps)),
            pltpu.SemaphoreType.DMA((CHUNKS, reps)),
            pltpu.SemaphoreType.DMA,
            pltpu.SemaphoreType.DMA,
            pltpu.SemaphoreType.DMA,
            pltpu.SemaphoreType.DMA,
        ],
        compiler_params=pltpu.CompilerParams(
            collective_id=0, has_side_effects=True, vmem_limit_bytes=56 * 1024 * 1024
        ),
    )(
        table,
        message,
        colloc,
        points.transpose(1, 0, 2),
        centers,
        exponents.reshape(1, -1),
        density.reshape(tiles, blk, blk),
    )
    return result.reshape(rows // reps, band, blk, blk)


def solution(mesh):
    in_specs = (
        P(AXES, None, None),
        P(AXES, None),
        P(AXES, None, None),
        P(None, "groups"),
        P("groups"),
        P(("groups", "batch", "block"), None, None, None),
    )
    out_specs = P(AXES, None, None, None)
    return jax.shard_map(
        per_device, mesh=mesh, in_specs=in_specs, out_specs=out_specs, check_vma=False
    )
```

```python
import functools

import jax
import jax.numpy as jnp
from jax import lax
from jax.experimental import pallas as pl
from jax.experimental.pallas import tpu as pltpu
from jax.sharding import PartitionSpec as P

TABLE_RATES = (0.5, 2.0)
TABLE_WEIGHTS = (1.0, 0.5)
MESH = pl.DeviceIdType.MESH
CHUNKS = 2
AXES = ("groups", "batch", "block", "rep")


def kernel(
    n_batch,
    n_block,
    reps,
    owners,
    capacity,
    band,
    blocks,
    message_in,
    colloc,
    points,
    centers,
    exponents,
    density,
    out,
    message,
    asked,
    asked_s,
    wanted,
    where,
    base,
    entry,
    functions,
    spots,
    mine,
    mirror,
    sending_side,
    sending_far,
    arrived,
    parts,
    returned_side,
    returned_far,
    sums,
    sums_own,
    far_in,
    rest,
    other,
    screens,
    overlap,
    flipped,
    gathered,
    field,
    colloc_v,
    ask_send,
    ask_recv,
    tile_send,
    tile_recv,
    back_send,
    back_recv,
    swap_send,
    swap_recv,
    out_send,
    out_recv,
    hand_send,
    hand_recv,
    colloc_sem,
    local_sem,
):
    group = lax.axis_index("groups")
    row = lax.axis_index("batch")
    col = lax.axis_index("block")
    rep = lax.axis_index("rep")
    depth = n_batch // 2
    side = row // depth
    far = 1 - side
    count = depth * n_block * reps
    me = ((row % depth) * n_block + col) * reps + rep
    batch_dev, pts, full = colloc.shape
    tiles, part, blk = mine.shape
    sub = part // CHUNKS
    listed = full // blk
    entries = batch_dev * listed
    width = capacity * listed
    kept = tiles // reps
    mine_rows = pl.ds(pl.multiple_of(rep * part, part), part)
    bf16 = jnp.bfloat16

    def device(p):
        chip = p // reps
        return (group, side * depth + chip // n_block, chip % n_block, p % reps)

    def across(c):
        return (group, far * depth + row % depth, col, c)

    partner = (group, row, col, 1 - rep)

    def peers(body):
        def step(k, carry):
            body(lax.rem(me + k, count))
            return carry

        lax.fori_loop(1, count, step, 0)

    load = pltpu.make_async_copy(density.at[:, mine_rows], mine, local_sem)
    load.start()
    load_colloc = pltpu.make_async_copy(colloc, colloc_v, colloc_sem)
    load_colloc.start()
    message[...] = jnp.zeros_like(message)
    message[0:batch_dev, 0:listed] = message_in[...]
    barrier = pltpu.get_barrier_semaphore()
    peers(lambda p: pl.semaphore_signal(barrier, inc=1, device_id=device(p), device_id_type=MESH))
    for c in range(reps):
        pl.semaphore_signal(barrier, inc=1, device_id=across(c), device_id_type=MESH)
    pl.semaphore_wait(barrier, count - 1 + reps)
    load.wait()

    def send(src, dst, out_sem, in_sem, where):
        return pltpu.make_async_remote_copy(
            src_ref=src,
            dst_ref=dst,
            send_sem=out_sem,
            recv_sem=in_sem,
            device_id=where,
            device_id_type=MESH,
        )

    def ask(p, slot):
        return send(
            message, asked.at[slot], ask_send.at[p], ask_recv.at[slot], device(p)
        )

    def packed(p, q):
        return sending_side.at[p] if q is None else sending_far.at[q, p]

    def mark(q):
        return 0 if q is None else 1 + q

    def span_of(q):
        return slice(0, part) if q is None else slice(q * sub, (q + 1) * sub)

    def serve(p, slot, q):
        first = (slot * 2 + (side if q is None else far)) * width
        span = span_of(q)
        return send(
            packed(p, q),
            arrived.at[pl.ds(first, width), pl.ds(span.start, span.stop - span.start)],
            tile_send.at[p, mark(q)],
            tile_recv.at[slot, mark(q)],
            device(p),
        )

    def give(p, slot, q):
        landing = returned_side if q is None else returned_far[q]
        return send(
            packed(p, q),
            landing.at[slot, pl.ds(0, width)],
            back_send.at[p, mark(q)],
            back_recv.at[slot, mark(q)],
            device(p),
        )

    def swap_in(q):
        return send(
            mine.at[:, pl.ds(q * sub, sub)],
            mirror[q],
            swap_send.at[q],
            swap_recv.at[q],
            across(rep),
        )

    def swap_out(q, c, source):
        return send(
            sums[q].at[pl.ds(c * kept, kept)],
            far_in.at[source, :, pl.ds(q * sub, sub)],
            out_send.at[q, c],
            out_recv.at[q, source],
            across(c),
        )

    peers(lambda p: ask(p, me).start())
    swap_in(0).start()
    own = pltpu.make_async_copy(message, asked.at[me], local_sem)
    own.start()
    own.wait()
    peers(lambda p: ask(p, p).wait_recv())
    to_scalar = pltpu.make_async_copy(asked, asked_s, local_sem)
    to_scalar.start()
    to_scalar.wait()

    def read(p, carry):
        lists = [[asked_s[p, b, j] for j in range(listed)] for b in range(batch_dev)]
        for role, batch_row in enumerate((row, far * depth + row % depth)):
            owner = batch_row * n_block + col
            taken = jnp.int32(0)
            slots = [[jnp.int32(-1)] * listed for _ in range(capacity)]
            for line in lists:
                for l in line:
                    local = lax.div(l, owners)
                    here = l - local * owners == owner
                    for k in range(capacity):
                        chosen = here & (taken == k)
                        for j in range(listed):
                            tile = local * band + (line[j] - l + band // 2)
                            slots[k][j] = jnp.where(chosen, tile, slots[k][j])
                    taken = taken + jnp.where(here, 1, 0)
            for k in range(capacity):
                for j in range(listed):
                    wanted[role, p, k * listed + j] = slots[k][j]
        return carry

    lax.fori_loop(0, count, read, 0)

    def send_tiles(q):
        role = 0 if q is None else 1
        h = side if q is None else far
        source = mine if q is None else mirror[q]
        span = span_of(q)

        def one(p):
            target = packed(p, q)
            for t in range(width):
                target[t] = source[jnp.maximum(wanted[role, p, t], 0)]
            serve(p, me, q).start()

        peers(one)
        for t in range(width):
            arrived[(me * 2 + h) * width + t, span] = source[jnp.maximum(wanted[role, me, t], 0)]

    send_tiles(None)

    def invert(p, carry):
        for role in range(2):
            slots = [wanted[role, p, t] for t in range(width)]
            for r in range(tiles):
                place = jnp.int32(width)
                for t in range(width):
                    place = jnp.where(slots[t] == r, t, place)
                where[role, p, r] = place
        return carry

    lax.fori_loop(0, count, invert, 0)

    flat = [blocks[b, j] for b in range(batch_dev) for j in range(listed)]
    targets = [l - lax.div(l, owners) * owners for l in flat]
    chips = owners // 2
    for e in range(entries):
        rank = jnp.int32(0)
        for earlier in range(e):
            rank = rank + jnp.where(targets[earlier] == targets[e], 1, 0)
        half = jnp.where(targets[e] >= chips, 1, 0)
        chip = targets[e] - half * chips
        base[e] = (chip * (2 * reps) + half) * width + rank * listed

    def fill(o, carry):
        taken = jnp.int32(0)
        held = [jnp.int32(0)] * capacity
        for e in range(entries):
            here = targets[e] == o
            for k in range(capacity):
                held[k] = jnp.where(here & (taken == k), e, held[k])
            taken = taken + jnp.where(here, 1, 0)
        for k in range(capacity):
            entry[o * capacity + k] = held[k]
        return carry

    lax.fori_loop(0, owners, fill, 0)

    def arrange(l, carry):
        lane = pl.ds(pl.multiple_of(l * blk, blk), blk)
        for k in range(3):
            functions[l, k : k + 1] = centers[k : k + 1, lane]
        functions[l, 3:4] = exponents[0:1, lane]
        return carry

    lax.fori_loop(0, functions.shape[0], arrange, 0)
    for b in range(batch_dev):
        for k in range(3):
            spots[b, k : k + 1] = points[k, b : b + 1]

    def column(line):
        return jnp.broadcast_to(line, (blk, blk)).T

    def prepare(b, carry):
        rows = []
        for i in range(listed):
            block = functions[blocks[b, i]]
            rows.append([block[k : k + 1] for k in range(4)])
        for i in range(listed):
            cols = [column(r) for r in rows[i]]
            for j in range(listed):
                dist = sum((cols[k] - rows[j][k]) * (cols[k] - rows[j][k]) for k in range(3))
                reduced = cols[3] * rows[j][3] / (cols[3] + rows[j][3])
                overlap[b, i * blk : (i + 1) * blk, j * blk : (j + 1) * blk] = jnp.exp(
                    -reduced * dist
                ).astype(bf16)
        rates = [
            [-(rows[j][3] * rate / (rows[j][3] + rate)) for rate in TABLE_RATES]
            for j in range(listed)
        ]

        def chunk(c, inner):
            lane = pl.ds(pl.multiple_of(c * blk, blk), blk)
            spot = [column(spots[b, k : k + 1, lane]) for k in range(3)]
            for j in range(listed):
                dist = sum((spot[k] - rows[j][k]) * (spot[k] - rows[j][k]) for k in range(3))
                for n in range(len(TABLE_RATES)):
                    screens[b, n, lane, j * blk : (j + 1) * blk] = jnp.exp(rates[j][n] * dist)
            return inner

        lax.fori_loop(0, pts // blk, chunk, 0)
        flipped[b] = colloc_v[b].T
        return carry

    load_colloc.wait()
    lax.fori_loop(0, batch_dev, prepare, 0)

    def blank(p, carry):
        returned_side[p, width] = jnp.zeros((part, blk), bf16)
        for q in range(CHUNKS):
            returned_far[q][p, width] = jnp.zeros((sub, blk), bf16)
        return carry

    lax.fori_loop(0, count, blank, 0)

    for q in range(CHUNKS):
        swap_in(q).wait_send()
        if q + 1 < CHUNKS:
            swap_in(q + 1).start()
        swap_in(q).wait_recv()
        send_tiles(q)
    for q in [None, *range(CHUNKS)]:
        peers(lambda p: serve(p, p, q).wait_recv())

    def build(b, carry):
        for i in range(listed):
            slot = base[b * listed + i]
            for j in range(listed):
                for c in range(reps):
                    top = i * blk + c * part
                    gathered[top : top + part, j * blk : (j + 1) * blk] = arrived[
                        slot + (2 * width * c + j)
                    ]
        step = min(256, pts)
        for c in range(pts // step):
            span = slice(c * step, (c + 1) * step)
            focused = (
                jnp.dot(colloc_v[b, span, :], gathered[...], preferred_element_type=jnp.float32)
                .astype(bf16)
                .astype(jnp.float32)
            )
            potential = None
            for n, weight in enumerate(TABLE_WEIGHTS):
                screen = screens[b, n, span, :]
                mixed = jnp.dot(
                    (screen * focused).astype(bf16), overlap[b], preferred_element_type=jnp.float32
                )
                term = weight * screen * mixed
                potential = term if potential is None else potential + term
            field[span, :] = potential.astype(bf16)
        for i in range(listed):
            block = jnp.dot(
                flipped[b, i * blk : (i + 1) * blk, :],
                field[...],
                preferred_element_type=jnp.float32,
            ).astype(bf16)
            for j in range(listed):
                for c in range(reps):
                    parts[((b * listed + i) * listed + j) * reps + c] = block[
                        c * part : (c + 1) * part, j * blk : (j + 1) * blk
                    ]
        return carry

    lax.fori_loop(0, batch_dev, build, 0)

    def send_back(q):
        h = side if q is None else far
        first = h * (count // reps) * capacity
        landing = returned_side if q is None else returned_far[q]
        span = span_of(q)

        def piece(p, k, j):
            number = entry[first + (p // reps) * capacity + k]
            return parts[number * (listed * reps) + (j * reps + p % reps)][span]

        def one(p):
            serve(p, me, q).wait_send()
            target = packed(p, q)
            for k in range(capacity):
                for j in range(listed):
                    target[k * listed + j] = piece(p, k, j)
            give(p, me, q).start()

        peers(one)
        for k in range(capacity):
            for j in range(listed):
                landing[me, k * listed + j] = piece(me, k, j)

    def total(r, q):
        role = 0 if q is None else 1
        landing = returned_side if q is None else returned_far[q]

        def add(p, running):
            return running + landing[p, where[role, p, r]].astype(jnp.float32)

        if count <= 8:
            running = add(0, 0.0)
            for p in range(1, count):
                running = add(p, running)
            return running
        return lax.fori_loop(0, count, add, jnp.zeros(landing.shape[2:], jnp.float32))

    send_back(0)
    for q in range(CHUNKS):
        peers(lambda p: give(p, me, q).wait_send())
        send_back(q + 1 if q + 1 < CHUNKS else None)
        peers(lambda p: give(p, p, q).wait_recv())

        def collect_far(r, carry):
            sums[q][r] = total(r, q).astype(bf16)
            return carry

        lax.fori_loop(0, tiles, collect_far, 0)
        for c in range(reps):
            swap_out(q, c, rep).start()

    peers(lambda p: give(p, p, None).wait_recv())

    def pass_on(r, carry):
        rest[r] = total((1 - rep) * kept + r, None).astype(bf16)
        return carry

    lax.fori_loop(0, kept, pass_on, 0)
    hand = send(rest, other, hand_send, hand_recv, partner)
    hand.start()

    def collect_own(r, carry):
        sums_own[r] = total(rep * kept + r, None)
        return carry

    lax.fori_loop(0, kept, collect_own, 0)
    hand.wait_recv()
    for q in range(CHUNKS):
        for c in range(reps):
            swap_out(q, c, c).wait_recv()
    other_rows = pl.ds(pl.multiple_of((1 - rep) * part, part), part)

    def finish(r, carry):
        out[r, mine_rows] = (sums_own[r] + far_in[rep, r].astype(jnp.float32)).astype(bf16)
        out[r, other_rows] = (
            other[r].astype(jnp.float32) + far_in[1 - rep, r].astype(jnp.float32)
        ).astype(bf16)
        return carry

    lax.fori_loop(0, kept, finish, 0)
    hand.wait_send()
    for q in range(CHUNKS):
        for c in range(reps):
            swap_out(q, c, rep).wait_send()
    peers(lambda p: ask(p, me).wait_send())
    peers(lambda p: give(p, me, None).wait_send())


def per_device(colloc, blocks, points, centers, exponents, density):
    n_batch, n_block, reps = (lax.axis_size(name) for name in AXES[1:])
    owners = n_batch * n_block
    batch_dev, listed = blocks.shape
    rows, band, blk, _ = density.shape
    pts, full = colloc.shape[1:]
    region = batch_dev * (band // 2 + 1)
    capacity = (region + owners - 1) // owners
    width = capacity * listed
    tiles = rows * band
    count = owners // 2 * reps
    part = blk // reps
    sub = part // CHUNKS
    kept = tiles // reps
    vmem = pl.BlockSpec(memory_space=pltpu.VMEM)
    bf16 = jnp.bfloat16
    result = pl.pallas_call(
        functools.partial(kernel, n_batch, n_block, reps, owners, capacity, band),
        out_shape=jax.ShapeDtypeStruct((tiles // reps, blk, blk), bf16),
        in_specs=[pl.BlockSpec(memory_space=pltpu.SMEM)]
        + [vmem, pl.BlockSpec(memory_space=pl.ANY)]
        + [vmem] * 3
        + [pl.BlockSpec(memory_space=pl.ANY)],
        out_specs=vmem,
        scratch_shapes=[
            pltpu.VMEM((8, 128), jnp.int32),
            pltpu.VMEM((count, 8, 128), jnp.int32),
            pltpu.SMEM((count, 8, 128), jnp.int32),
            pltpu.SMEM((2, count, width), jnp.int32),
            pltpu.SMEM((2, count, tiles), jnp.int32),
            pltpu.SMEM((batch_dev * listed,), jnp.int32),
            pltpu.SMEM((owners * capacity,), jnp.int32),
            pltpu.VMEM((centers.shape[1] // blk, 4, blk), jnp.float32),
            pltpu.VMEM((batch_dev, 3, pts), jnp.float32),
            pltpu.VMEM((tiles, part, blk), bf16),
            tuple(pltpu.VMEM((tiles, sub, blk), bf16) for _ in range(CHUNKS)),
            pltpu.VMEM((count, width, part, blk), bf16),
            pltpu.VMEM((CHUNKS, count, width, sub, blk), bf16),
            pltpu.VMEM((count * 2 * width, part, blk), bf16),
            pltpu.VMEM((batch_dev * listed * listed * reps, part, blk), bf16),
            pltpu.VMEM((count, width + 1, part, blk), bf16),
            tuple(pltpu.VMEM((count, width + 1, sub, blk), bf16) for _ in range(CHUNKS)),
            tuple(pltpu.VMEM((tiles, sub, blk), bf16) for _ in range(CHUNKS)),
            pltpu.VMEM((kept, part, blk), jnp.float32),
            pltpu.VMEM((reps, kept, part, blk), bf16),
            pltpu.VMEM((kept, part, blk), bf16),
            pltpu.VMEM((kept, part, blk), bf16),
            pltpu.VMEM((batch_dev, len(TABLE_RATES), pts, full), jnp.float32),
            pltpu.VMEM((batch_dev, full, full), bf16),
            pltpu.VMEM((batch_dev, full, pts), bf16),
            pltpu.VMEM((full, full), bf16),
            pltpu.VMEM((pts, full), bf16),
            pltpu.VMEM(colloc.shape, bf16),
            pltpu.SemaphoreType.DMA((count,)),
            pltpu.SemaphoreType.DMA((count,)),
            pltpu.SemaphoreType.DMA((count, 1 + CHUNKS)),
            pltpu.SemaphoreType.DMA((count, 1 + CHUNKS)),
            pltpu.SemaphoreType.DMA((count, 1 + CHUNKS)),
            pltpu.SemaphoreType.DMA((count, 1 + CHUNKS)),
            pltpu.SemaphoreType.DMA((CHUNKS,)),
            pltpu.SemaphoreType.DMA((CHUNKS,)),
            pltpu.SemaphoreType.DMA((CHUNKS, reps)),
            pltpu.SemaphoreType.DMA((CHUNKS, reps)),
            pltpu.SemaphoreType.DMA,
            pltpu.SemaphoreType.DMA,
            pltpu.SemaphoreType.DMA,
            pltpu.SemaphoreType.DMA,
        ],
        compiler_params=pltpu.CompilerParams(
            collective_id=0, has_side_effects=True, vmem_limit_bytes=56 * 1024 * 1024
        ),
    )(
        blocks,
        blocks,
        colloc,
        points.transpose(1, 0, 2),
        centers,
        exponents.reshape(1, -1),
        density.reshape(tiles, blk, blk),
    )
    return result.reshape(rows // reps, band, blk, blk)


def solution(mesh):
    in_specs = (
        P(AXES, None, None),
        P(AXES, None),
        P(AXES, None, None),
        P(None, "groups"),
        P("groups"),
        P(("groups", "batch", "block"), None, None, None),
    )
    out_specs = P(AXES, None, None, None)
    return jax.shard_map(
        per_device, mesh=mesh, in_specs=in_specs, out_specs=out_specs, check_vma=False
    )
```

```python
import functools

import jax
import jax.numpy as jnp
from jax import lax
from jax.experimental import pallas as pl
from jax.experimental.pallas import tpu as pltpu
from jax.sharding import PartitionSpec as P

TABLE_RATES = (0.5, 2.0)
TABLE_WEIGHTS = (1.0, 0.5)
MESH = pl.DeviceIdType.MESH
CHUNKS = 2
AXES = ("groups", "batch", "block", "rep")


def kernel(
    n_batch,
    n_block,
    reps,
    owners,
    capacity,
    band,
    blocks,
    message_in,
    colloc,
    points,
    centers,
    exponents,
    density,
    out,
    out_far,
    message,
    asked,
    asked_s,
    wanted,
    where,
    base,
    entry,
    functions,
    spots,
    mine,
    mirror,
    sending_side,
    sending_far,
    arrived,
    parts,
    returned_side,
    returned_far,
    sums,
    far_in,
    rest,
    other,
    screens,
    overlap,
    flipped,
    gathered,
    field,
    colloc_v,
    ask_send,
    ask_recv,
    tile_send,
    tile_recv,
    back_send,
    back_recv,
    swap_send,
    swap_recv,
    out_send,
    out_recv,
    hand_send,
    hand_recv,
    colloc_sem,
    local_sem,
):
    group = lax.axis_index("groups")
    row = lax.axis_index("batch")
    col = lax.axis_index("block")
    rep = lax.axis_index("rep")
    depth = n_batch // 2
    side = row // depth
    far = 1 - side
    count = depth * n_block * reps
    me = ((row % depth) * n_block + col) * reps + rep
    batch_dev, pts, full = colloc.shape
    tiles, part, blk = mine.shape
    sub = part // CHUNKS
    listed = full // blk
    entries = batch_dev * listed
    width = capacity * listed
    kept = tiles // reps
    mine_rows = pl.ds(pl.multiple_of(rep * part, part), part)
    bf16 = jnp.bfloat16

    def device(p):
        chip = p // reps
        return (group, side * depth + chip // n_block, chip % n_block, p % reps)

    def across(c):
        return (group, far * depth + row % depth, col, c)

    partner = (group, row, col, 1 - rep)

    def peers(body):
        def step(k, carry):
            body(lax.rem(me + k, count))
            return carry

        lax.fori_loop(1, count, step, 0)

    load = pltpu.make_async_copy(density.at[:, mine_rows], mine, local_sem)
    load.start()
    load_colloc = pltpu.make_async_copy(colloc, colloc_v, colloc_sem)
    load_colloc.start()
    message[...] = jnp.zeros_like(message)
    message[0:batch_dev, 0:listed] = message_in[...]
    barrier = pltpu.get_barrier_semaphore()
    peers(lambda p: pl.semaphore_signal(barrier, inc=1, device_id=device(p), device_id_type=MESH))
    for c in range(reps):
        pl.semaphore_signal(barrier, inc=1, device_id=across(c), device_id_type=MESH)
    pl.semaphore_wait(barrier, count - 1 + reps)
    load.wait()

    def send(src, dst, out_sem, in_sem, where):
        return pltpu.make_async_remote_copy(
            src_ref=src,
            dst_ref=dst,
            send_sem=out_sem,
            recv_sem=in_sem,
            device_id=where,
            device_id_type=MESH,
        )

    def ask(p, slot):
        return send(
            message, asked.at[slot], ask_send.at[p], ask_recv.at[slot], device(p)
        )

    def packed(p, q):
        return sending_side.at[p] if q is None else sending_far.at[q, p]

    def mark(q):
        return 0 if q is None else 1 + q

    def span_of(q):
        return slice(0, part) if q is None else slice(q * sub, (q + 1) * sub)

    def serve(p, slot, q):
        first = (slot * 2 + (side if q is None else far)) * width
        span = span_of(q)
        return send(
            packed(p, q),
            arrived.at[pl.ds(first, width), pl.ds(span.start, span.stop - span.start)],
            tile_send.at[p, mark(q)],
            tile_recv.at[slot, mark(q)],
            device(p),
        )

    def give(p, slot, q):
        landing = returned_side if q is None else returned_far[q]
        return send(
            packed(p, q),
            landing.at[slot, pl.ds(0, width)],
            back_send.at[p, mark(q)],
            back_recv.at[slot, mark(q)],
            device(p),
        )

    def swap_in(q):
        return send(
            mine.at[:, pl.ds(q * sub, sub)],
            mirror[q],
            swap_send.at[q],
            swap_recv.at[q],
            across(rep),
        )

    def swap_out(q, c, source):
        return send(
            sums[q].at[pl.ds(c * kept, kept)],
            far_in.at[source, :, pl.ds(q * sub, sub)],
            out_send.at[q, c],
            out_recv.at[q, source],
            across(c),
        )

    peers(lambda p: ask(p, me).start())
    swap_in(0).start()
    own = pltpu.make_async_copy(message, asked.at[me], local_sem)
    own.start()
    own.wait()
    peers(lambda p: ask(p, p).wait_recv())
    to_scalar = pltpu.make_async_copy(asked, asked_s, local_sem)
    to_scalar.start()
    to_scalar.wait()

    def read(p, carry):
        lists = [[asked_s[p, b, j] for j in range(listed)] for b in range(batch_dev)]
        for role, batch_row in enumerate((row, far * depth + row % depth)):
            owner = batch_row * n_block + col
            taken = jnp.int32(0)
            slots = [[jnp.int32(-1)] * listed for _ in range(capacity)]
            for line in lists:
                for l in line:
                    local = lax.div(l, owners)
                    here = l - local * owners == owner
                    for k in range(capacity):
                        chosen = here & (taken == k)
                        for j in range(listed):
                            tile = local * band + (line[j] - l + band // 2)
                            slots[k][j] = jnp.where(chosen, tile, slots[k][j])
                    taken = taken + jnp.where(here, 1, 0)
            for k in range(capacity):
                for j in range(listed):
                    wanted[role, p, k * listed + j] = slots[k][j]
        return carry

    lax.fori_loop(0, count, read, 0)

    def send_tiles(q):
        role = 0 if q is None else 1
        h = side if q is None else far
        source = mine if q is None else mirror[q]
        span = span_of(q)

        def one(p):
            target = packed(p, q)
            for t in range(width):
                target[t] = source[jnp.maximum(wanted[role, p, t], 0)]
            serve(p, me, q).start()

        peers(one)
        for t in range(width):
            arrived[(me * 2 + h) * width + t, span] = source[jnp.maximum(wanted[role, me, t], 0)]

    send_tiles(None)

    def invert(p, carry):
        for role in range(2):
            slots = [wanted[role, p, t] for t in range(width)]
            for r in range(tiles):
                place = jnp.int32(width)
                for t in range(width):
                    place = jnp.where(slots[t] == r, t, place)
                where[role, p, r] = place
        return carry

    lax.fori_loop(0, count, invert, 0)

    flat = [blocks[b, j] for b in range(batch_dev) for j in range(listed)]
    targets = [l - lax.div(l, owners) * owners for l in flat]
    chips = owners // 2
    for e in range(entries):
        rank = jnp.int32(0)
        for earlier in range(e):
            rank = rank + jnp.where(targets[earlier] == targets[e], 1, 0)
        half = jnp.where(targets[e] >= chips, 1, 0)
        chip = targets[e] - half * chips
        base[e] = (chip * (2 * reps) + half) * width + rank * listed

    def fill(o, carry):
        taken = jnp.int32(0)
        held = [jnp.int32(0)] * capacity
        for e in range(entries):
            here = targets[e] == o
            for k in range(capacity):
                held[k] = jnp.where(here & (taken == k), e, held[k])
            taken = taken + jnp.where(here, 1, 0)
        for k in range(capacity):
            entry[o * capacity + k] = held[k]
        return carry

    lax.fori_loop(0, owners, fill, 0)

    def arrange(l, carry):
        lane = pl.ds(pl.multiple_of(l * blk, blk), blk)
        for k in range(3):
            functions[l, k : k + 1] = centers[k : k + 1, lane]
        functions[l, 3:4] = exponents[0:1, lane]
        return carry

    lax.fori_loop(0, functions.shape[0], arrange, 0)
    for b in range(batch_dev):
        for k in range(3):
            spots[b, k : k + 1] = points[k, b : b + 1]

    def column(line):
        return jnp.broadcast_to(line, (blk, blk)).T

    def prepare(b, carry):
        rows = []
        for i in range(listed):
            block = functions[blocks[b, i]]
            rows.append([block[k : k + 1] for k in range(4)])
        for i in range(listed):
            cols = [column(r) for r in rows[i]]
            for j in range(listed):
                dist = sum((cols[k] - rows[j][k]) * (cols[k] - rows[j][k]) for k in range(3))
                reduced = cols[3] * rows[j][3] / (cols[3] + rows[j][3])
                overlap[b, i * blk : (i + 1) * blk, j * blk : (j + 1) * blk] = jnp.exp(
                    -reduced * dist
                ).astype(bf16)
        rates = [
            [-(rows[j][3] * rate / (rows[j][3] + rate)) for rate in TABLE_RATES]
            for j in range(listed)
        ]

        def chunk(c, inner):
            lane = pl.ds(pl.multiple_of(c * blk, blk), blk)
            spot = [column(spots[b, k : k + 1, lane]) for k in range(3)]
            for j in range(listed):
                dist = sum((spot[k] - rows[j][k]) * (spot[k] - rows[j][k]) for k in range(3))
                for n in range(len(TABLE_RATES)):
                    screens[b, n, lane, j * blk : (j + 1) * blk] = jnp.exp(rates[j][n] * dist)
            return inner

        lax.fori_loop(0, pts // blk, chunk, 0)
        flipped[b] = colloc_v[b].T
        return carry

    load_colloc.wait()
    lax.fori_loop(0, batch_dev, prepare, 0)

    def blank(p, carry):
        returned_side[p, width] = jnp.zeros((part, blk), bf16)
        for q in range(CHUNKS):
            returned_far[q][p, width] = jnp.zeros((sub, blk), bf16)
        return carry

    lax.fori_loop(0, count, blank, 0)

    for q in range(CHUNKS):
        swap_in(q).wait_send()
        if q + 1 < CHUNKS:
            swap_in(q + 1).start()
        swap_in(q).wait_recv()
        send_tiles(q)
    for q in [None, *range(CHUNKS)]:
        peers(lambda p: serve(p, p, q).wait_recv())

    def build(b, carry):
        for i in range(listed):
            slot = base[b * listed + i]
            for j in range(listed):
                for c in range(reps):
                    top = i * blk + c * part
                    gathered[top : top + part, j * blk : (j + 1) * blk] = arrived[
                        slot + (2 * width * c + j)
                    ]
        step = min(256, pts)
        for c in range(pts // step):
            span = slice(c * step, (c + 1) * step)
            focused = (
                jnp.dot(colloc_v[b, span, :], gathered[...], preferred_element_type=jnp.float32)
                .astype(bf16)
                .astype(jnp.float32)
            )
            potential = None
            for n, weight in enumerate(TABLE_WEIGHTS):
                screen = screens[b, n, span, :]
                mixed = jnp.dot(
                    (screen * focused).astype(bf16), overlap[b], preferred_element_type=jnp.float32
                )
                term = weight * screen * mixed
                potential = term if potential is None else potential + term
            field[span, :] = potential.astype(bf16)
        for i in range(listed):
            block = jnp.dot(
                flipped[b, i * blk : (i + 1) * blk, :],
                field[...],
                preferred_element_type=jnp.float32,
            ).astype(bf16)
            for j in range(listed):
                for c in range(reps):
                    parts[((b * listed + i) * listed + j) * reps + c] = block[
                        c * part : (c + 1) * part, j * blk : (j + 1) * blk
                    ]
        return carry

    lax.fori_loop(0, batch_dev, build, 0)

    def send_back(q):
        h = side if q is None else far
        first = h * (count // reps) * capacity
        landing = returned_side if q is None else returned_far[q]
        span = span_of(q)

        def piece(p, k, j):
            number = entry[first + (p // reps) * capacity + k]
            return parts[number * (listed * reps) + (j * reps + p % reps)][span]

        def one(p):
            serve(p, me, q).wait_send()
            target = packed(p, q)
            for k in range(capacity):
                for j in range(listed):
                    target[k * listed + j] = piece(p, k, j)
            give(p, me, q).start()

        peers(one)
        for k in range(capacity):
            for j in range(listed):
                landing[me, k * listed + j] = piece(me, k, j)

    def total(r, q):
        role = 0 if q is None else 1
        landing = returned_side if q is None else returned_far[q]

        def add(p, running):
            return running + landing[p, where[role, p, r]].astype(jnp.float32)

        if count <= 8:
            running = add(0, 0.0)
            for p in range(1, count):
                running = add(p, running)
            return running
        return lax.fori_loop(0, count, add, jnp.zeros(landing.shape[2:], jnp.float32))

    send_back(0)
    for q in range(CHUNKS):
        peers(lambda p: give(p, me, q).wait_send())
        send_back(q + 1 if q + 1 < CHUNKS else None)
        peers(lambda p: give(p, p, q).wait_recv())

        def collect_far(r, carry):
            sums[q][r] = total(r, q).astype(bf16)
            return carry

        lax.fori_loop(0, tiles, collect_far, 0)
        for c in range(reps):
            swap_out(q, c, rep).start()

    peers(lambda p: give(p, p, None).wait_recv())

    def pass_on(r, carry):
        rest[r] = total((1 - rep) * kept + r, None).astype(bf16)
        return carry

    lax.fori_loop(0, kept, pass_on, 0)
    hand = send(rest, other, hand_send, hand_recv, partner)
    hand.start()

    def collect_own(r, carry):
        out[r, mine_rows] = total(rep * kept + r, None).astype(bf16)
        return carry

    lax.fori_loop(0, kept, collect_own, 0)
    hand.wait_recv()
    other_rows = pl.ds(pl.multiple_of((1 - rep) * part, part), part)

    def take(r, carry):
        out[r, other_rows] = other[r]
        return carry

    lax.fori_loop(0, kept, take, 0)
    for q in range(CHUNKS):
        for c in range(reps):
            swap_out(q, c, c).wait_recv()

    def finish(r, carry):
        for c in range(reps):
            out_far[r, c * part : (c + 1) * part] = far_in[c, r]
        return carry

    lax.fori_loop(0, kept, finish, 0)
    hand.wait_send()
    for q in range(CHUNKS):
        for c in range(reps):
            swap_out(q, c, rep).wait_send()
    peers(lambda p: ask(p, me).wait_send())
    peers(lambda p: give(p, me, None).wait_send())


def per_device(colloc, blocks, points, centers, exponents, density):
    n_batch, n_block, reps = (lax.axis_size(name) for name in AXES[1:])
    owners = n_batch * n_block
    batch_dev, listed = blocks.shape
    rows, band, blk, _ = density.shape
    pts, full = colloc.shape[1:]
    region = batch_dev * (band // 2 + 1)
    capacity = (region + owners - 1) // owners
    width = capacity * listed
    tiles = rows * band
    count = owners // 2 * reps
    part = blk // reps
    sub = part // CHUNKS
    kept = tiles // reps
    vmem = pl.BlockSpec(memory_space=pltpu.VMEM)
    bf16 = jnp.bfloat16
    here, away = pl.pallas_call(
        functools.partial(kernel, n_batch, n_block, reps, owners, capacity, band),
        out_shape=[jax.ShapeDtypeStruct((tiles // reps, blk, blk), bf16)] * 2,
        in_specs=[pl.BlockSpec(memory_space=pltpu.SMEM)]
        + [vmem, pl.BlockSpec(memory_space=pl.ANY)]
        + [vmem] * 3
        + [pl.BlockSpec(memory_space=pl.ANY)],
        out_specs=[vmem, vmem],
        scratch_shapes=[
            pltpu.VMEM((8, 128), jnp.int32),
            pltpu.VMEM((count, 8, 128), jnp.int32),
            pltpu.SMEM((count, 8, 128), jnp.int32),
            pltpu.SMEM((2, count, width), jnp.int32),
            pltpu.SMEM((2, count, tiles), jnp.int32),
            pltpu.SMEM((batch_dev * listed,), jnp.int32),
            pltpu.SMEM((owners * capacity,), jnp.int32),
            pltpu.VMEM((centers.shape[1] // blk, 4, blk), jnp.float32),
            pltpu.VMEM((batch_dev, 3, pts), jnp.float32),
            pltpu.VMEM((tiles, part, blk), bf16),
            tuple(pltpu.VMEM((tiles, sub, blk), bf16) for _ in range(CHUNKS)),
            pltpu.VMEM((count, width, part, blk), bf16),
            pltpu.VMEM((CHUNKS, count, width, sub, blk), bf16),
            pltpu.VMEM((count * 2 * width, part, blk), bf16),
            pltpu.VMEM((batch_dev * listed * listed * reps, part, blk), bf16),
            pltpu.VMEM((count, width + 1, part, blk), bf16),
            tuple(pltpu.VMEM((count, width + 1, sub, blk), bf16) for _ in range(CHUNKS)),
            tuple(pltpu.VMEM((tiles, sub, blk), bf16) for _ in range(CHUNKS)),
            pltpu.VMEM((reps, kept, part, blk), bf16),
            pltpu.VMEM((kept, part, blk), bf16),
            pltpu.VMEM((kept, part, blk), bf16),
            pltpu.VMEM((batch_dev, len(TABLE_RATES), pts, full), jnp.float32),
            pltpu.VMEM((batch_dev, full, full), bf16),
            pltpu.VMEM((batch_dev, full, pts), bf16),
            pltpu.VMEM((full, full), bf16),
            pltpu.VMEM((pts, full), bf16),
            pltpu.VMEM(colloc.shape, bf16),
            pltpu.SemaphoreType.DMA((count,)),
            pltpu.SemaphoreType.DMA((count,)),
            pltpu.SemaphoreType.DMA((count, 1 + CHUNKS)),
            pltpu.SemaphoreType.DMA((count, 1 + CHUNKS)),
            pltpu.SemaphoreType.DMA((count, 1 + CHUNKS)),
            pltpu.SemaphoreType.DMA((count, 1 + CHUNKS)),
            pltpu.SemaphoreType.DMA((CHUNKS,)),
            pltpu.SemaphoreType.DMA((CHUNKS,)),
            pltpu.SemaphoreType.DMA((CHUNKS, reps)),
            pltpu.SemaphoreType.DMA((CHUNKS, reps)),
            pltpu.SemaphoreType.DMA,
            pltpu.SemaphoreType.DMA,
            pltpu.SemaphoreType.DMA,
            pltpu.SemaphoreType.DMA,
        ],
        compiler_params=pltpu.CompilerParams(
            collective_id=0, has_side_effects=True, vmem_limit_bytes=56 * 1024 * 1024
        ),
    )(
        blocks,
        blocks,
        colloc,
        points.transpose(1, 0, 2),
        centers,
        exponents.reshape(1, -1),
        density.reshape(tiles, blk, blk),
    )
    result = (here.astype(jnp.float32) + away.astype(jnp.float32)).astype(bf16)
    return result.reshape(rows // reps, band, blk, blk)


def solution(mesh):
    in_specs = (
        P(AXES, None, None),
        P(AXES, None),
        P(AXES, None, None),
        P(None, "groups"),
        P("groups"),
        P(("groups", "batch", "block"), None, None, None),
    )
    out_specs = P(AXES, None, None, None)
    return jax.shard_map(
        per_device, mesh=mesh, in_specs=in_specs, out_specs=out_specs, check_vma=False
    )
```
